128 devices in a mesh: dp: 4 (over y_lo, core), ep: 32 (over x, y_hi, z).
Axes of the slice: x: 4, y: 4 (y_hi: 2, y_lo: 2; y = y_hi * 2 + y_lo), z: 4, core: 2. Of those that a mesh axis runs over, the one named last changes fastest.
Arguments:
- latent_pool: bfloat16 [16384, 36864], P(('dp', 'ep')), may hold values from -6 to 6
- queries: bfloat16 [2048, 73728], P(('dp', 'ep')), may hold values from -72 to 72, as said below
- hidden: bfloat16 [2048, 7168], P(('dp', 'ep')), may hold values from -6 to 6
- lengths: int32 [128, 16], P(('dp', 'ep')), may hold values from 1 to 512, 5120 in all within a row
- page_table: int32 [128, 128], P(('dp', 'ep')), may hold values from 0 to 127, each once within a row
- send_slot: int32 [128, 2], P(('dp', 'ep')), may hold values from 0 to 15, as said below
- match: int32 [32, 2], P('ep'), may hold values from 1 to 3
- routes: int32 [2048, 8], P(('dp', 'ep')), may hold values from 0 to 31, all different within a row; in each aligned block of 16 rows (0 to 15, 16 to 31, ...) at most 8 rows name the same one
- route_gain: int32 [2048, 8], P(('dp', 'ep')), may hold values from 1 to 16
- w_gate: bfloat16 [32, 7168, 1024], P('ep', None, 'dp'), may hold values from -0.0625 to 0.0625
- w_up: bfloat16 [32, 7168, 1024], P('ep', None, 'dp'), may hold values from -0.0625 to 0.0625
- w_down: bfloat16 [32, 1024, 7168], P('ep', 'dp'), may hold values from -0.1875 to 0.1875
Outputs:
- attn_context: bfloat16 [2048, 65536], P(('dp', 'ep'))
- moe_out: bfloat16 [2048, 7168], P(('dp', 'ep'))
The draws below stay inside these ranges and needn't reach their ends.
Inputs may be any that keep to these rules, and one draw needn't show every extreme that they name: queries are finite. `send_slot`: the 2 slots listed for one device are different. `match`: a swap's partner replica is the replica index xor this value; it is the same for all replicas of one ep index. `routes`: each row names 8 different experts; among the 16 rows of one device no expert is named by more than 8 rows, a bound that some block reaches. `page_table`: the slot s request's pages are entries s * 8 to s * 8 + 7 of its device's row, in logical order; each row is a permutation.
All inputs are finite; a program needn't handle non-finite values.
Results may differ from the reference program's by a relative error of at most 0.015.
Values may be sent and summed in bfloat16 or wider, within the bound.
No kernel may reach another device: no remote copies, remote signals or barrier semaphores. Data moves between devices by JAX's collectives and lax.ppermute only.
A program may use at most 192 MiB of HBM per device.

```python
import math
import jax
import jax.numpy as jnp
import numpy as np
from jax import lax

D = 7168
HEADS = 128
LATENT = 512
KV = 576
FF_DEV = 256
FF = 1024
TOP = 8
PAGE = 64
MAXPAGES = 8
REQ_DEV = 16
SWAPS = 2
DEVS = 128
TOKENS = 2048
PAGES = 128
EXPERTS = 32
CAP = 8
N_DP = 4
N_EP = 32


def draw_queries(key, part):
    key = jax.random.fold_in(key, 11)
    shape = (N_DP * N_EP * REQ_DEV, HEADS, KV)
    values = jnp.clip(jax.random.normal(key, shape, jnp.float32), -6.0, 6.0)
    return values.reshape(N_DP * N_EP * REQ_DEV, HEADS * KV).astype(jnp.bfloat16)


def draw_send_slot(key, part):
    key = jax.random.fold_in(key, 23)
    subkeys = jax.random.split(key, N_DP * N_EP)
    return jax.vmap(lambda subkey: jax.random.permutation(subkey, REQ_DEV)[:SWAPS])(subkeys).astype(jnp.int32)


def set_ends(entries, stream_key, smallest, top_value):
    longest = entries.shape.index(max(entries.shape))
    spots = []
    for shift in (0, 1):
        where = [jax.random.randint(jax.random.fold_in(stream_key, axis), (), 0, length) for axis, length in enumerate(entries.shape)]
        where[longest] = (where[longest] + shift) % entries.shape[longest]
        spots.append(tuple(where))
    return entries.at[spots[0]].set(smallest).at[spots[1]].set(top_value)


def block_scale(rng, dims, pieces, least, largest):
    loudness, own = 1.0, jax.random.fold_in(rng, 6)
    for axis_at, blocks in pieces:
        steps = jnp.exp(jax.random.uniform(jax.random.fold_in(own, axis_at), (blocks,), jnp.float32, least / len(pieces), largest / len(pieces)))
        loudness = loudness * jnp.repeat(steps, dims[axis_at] // blocks).reshape([-1 if axis == axis_at else 1 for axis in range(len(dims))])
    return loudness


def profile(count, total, most, lean):
    portions = [(1 << 20) // math.isqrt(rank ** lean) + 1 for rank in range(2, count + 1)]
    rest, counts = total - most - (count - 1), [1] * (count - 1)
    while rest > 0:
        free = [i for i in range(count - 1) if counts[i] < most]
        pool, left = sum([portions[i] for i in free]), rest
        for i in free:
            extra = min(most - counts[i], max(1, left * portions[i] // pool), rest)
            counts[i] = counts[i] + extra
            rest = rest - extra
    return np.array([most] + counts)


def ragged(stream_key, count, total, reach, skew):
    if count == 2:
        one = jax.random.randint(stream_key, (), max(1, total - reach), min(reach, total - 1) + 1)
        return jnp.stack([one, total - one])
    sizes = jnp.asarray(profile(count, total, reach, skew), jnp.int32)
    twos = (count - 1) // 2
    donor, taker = sizes[1:1 + 2 * twos:2], sizes[2:2 + 2 * twos:2]
    margin = jnp.minimum(donor - 1, reach - taker)
    shifted = jax.random.randint(jax.random.fold_in(stream_key, 1), (twos,), 0, 1 << 20) % (margin + 1)
    sizes = sizes.at[1:1 + 2 * twos:2].set(donor - shifted).at[2:2 + 2 * twos:2].set(taker + shifted)
    return sizes[jax.random.permutation(jax.random.fold_in(stream_key, 2), count)]


def assign_block(stream_key, own, number, rows, number_of, top, bound, lean):
    ranking = jax.random.permutation(stream_key, number_of)
    packed, ordinary = portions_of(number_of, rows * top, bound, lean, True), portions_of(number_of, rows * top, bound, lean, False)
    places = jnp.arange(number_of)

    def named(sizes, turn):
        used = int((sizes > 0).sum())
        fixed = max(1, used // 4)
        passed = fixed + (places - fixed + turn * (used - fixed)) % max(1, number_of - fixed)
        return jnp.zeros((number_of,), jnp.int32).at[ranking[jnp.where(places < fixed, places, passed)]].set(jnp.asarray(sizes, jnp.int32))

    sizes = jnp.where(number % 4 == 0, named(packed, number // 4), named(ordinary, number - number // 4 - 1))
    mixed = jax.random.permutation(jax.random.fold_in(own, 3), number_of)
    source_of, taker = mixed[0:number_of // 2 * 2:2], mixed[1:number_of // 2 * 2:2]
    slack = jnp.minimum(sizes[source_of] - 1, bound - sizes[taker]) // 2
    slack = jnp.where((source_of == ranking[0]) | (taker == ranking[0]) | (sizes[taker] == 0), 0, jnp.maximum(slack, 0))
    passed = jax.random.randint(jax.random.fold_in(own, 4), (number_of // 2,), 0, 1 << 20) % (slack + 1)
    sizes = sizes.at[source_of].add(-passed).at[taker].add(passed)
    labels = jnp.searchsorted(jnp.cumsum(sizes), jnp.arange(rows * top), side="right").astype(jnp.int32)
    table = labels.reshape(top, rows).T
    table = table[jax.random.permutation(jax.random.fold_in(own, 1), rows)]
    turn = jax.random.randint(jax.random.fold_in(own, 2), (rows, 1), 0, top)
    return jnp.take_along_axis(table, (jnp.arange(top)[None, :] + turn) % top, axis=1)


def portions_of(number_of, total, limit, lean, full):
    weights = [(1 << 20) // math.isqrt(rank ** lean) + 1 for rank in range(1, number_of + 1)]
    largest = limit if full else min(limit, max(-(-total // number_of), total * weights[0] // sum(weights)))
    least = 1 if total - largest >= number_of - 1 else 0
    holding, rest = [largest] + [least] * (number_of - 1), total - largest - least * (number_of - 1)
    while rest > 0:
        free = [i for i in range(1, number_of) if holding[i] < largest] or [i for i in range(1, number_of) if holding[i] < limit]
        whole, remaining = sum([weights[i] for i in free]), rest
        for i in free:
            addition = min(limit - holding[i], max(1, remaining * weights[i] // whole), rest)
            holding[i] = holding[i] + addition
            rest = rest - addition
    return np.array(holding)


def scatter_about(rng, extent, spread, bound, shards=(), held_as=jnp.bfloat16):
    array = jax.random.normal(rng, extent, jnp.float32) * spread
    if len(shards) > 0:
        array = block_scale(rng, extent, shards, -0.22, 0.18) * array
    return jnp.clip(array, min=-bound, max=bound).astype(held_as)


def setup_inputs(seed: int = 0) -> dict:
    key_list = jax.random.split(jax.random.key(seed), 13)
    latent_pool = scatter_about(key_list[0], (DEVS * PAGES, PAGE * KV), 1.0, 6.0, ((0, 128),))
    queries = draw_queries(jax.random.fold_in(key_list[12], 71), 0)
    hidden = scatter_about(key_list[2], (TOKENS, D), 1.0, 6.0, ((0, 128),))
    lengths = jax.vmap(lambda own: ragged(own, REQ_DEV, REQ_DEV * MAXPAGES * PAGE * 5 // 8, MAXPAGES * PAGE, 2))(jax.random.split(key_list[3], DEVS)).reshape((DEVS, REQ_DEV)).astype(jnp.int32)
    page_table = jax.vmap(lambda own: jax.random.permutation(own, PAGES))(jax.random.split(key_list[4], DEVS)).reshape((DEVS, PAGES)).astype(jnp.int32)
    send_slot = draw_send_slot(jax.random.fold_in(key_list[12], 71), 0)
    match = set_ends(jax.random.randint(key_list[6], (N_EP, SWAPS), 1, N_DP), jax.random.fold_in(key_list[6], 1), 1, N_DP - 1).astype(jnp.int32)
    routes_keys = jax.random.split(jax.random.fold_in(key_list[7], 1), TOKENS // REQ_DEV)
    routes_turns = jax.random.permutation(jax.random.fold_in(key_list[7], 3), TOKENS // REQ_DEV)
    routes = jax.vmap(lambda own, number: assign_block(jax.random.fold_in(key_list[7], 2), own, number, REQ_DEV, EXPERTS, TOP, CAP, 2))(routes_keys, routes_turns).reshape((TOKENS, TOP))
    route_gain = set_ends(jax.random.randint(key_list[8], (TOKENS, TOP), 1, 17), jax.random.fold_in(key_list[8], 1), 1, 16).astype(jnp.int32)
    w_gate = scatter_about(key_list[9], (EXPERTS, D, FF), D ** -0.5, 0.0625, ((0, 32), (2, 4)))
    w_up = scatter_about(key_list[10], (EXPERTS, D, FF), D ** -0.5, 0.0625, ((0, 32), (2, 4)))
    w_down = scatter_about(key_list[11], (EXPERTS, FF, D), FF ** -0.5, 0.1875, ((0, 32), (1, 4)))
    return dict(latent_pool=latent_pool, queries=queries, hidden=hidden, lengths=lengths, page_table=page_table, send_slot=send_slot, match=match, routes=routes, route_gain=route_gain, w_gate=w_gate, w_up=w_up, w_down=w_down)


score_scale = 192.0 ** -0.5
gain_step = 0.0625


def source_rows(send_slot, match):
    device_ids = jnp.arange(N_DP * N_EP, dtype=jnp.int32)
    replica = device_ids // N_EP
    column = device_ids % N_EP
    partner = jnp.bitwise_xor(replica[:, None], match[column]) * N_EP + column[:, None]
    partner_slot = send_slot[partner, jnp.arange(SWAPS, dtype=jnp.int32)[None, :]]
    from_device = jnp.broadcast_to(device_ids[:, None], (N_DP * N_EP, REQ_DEV))
    from_slot = jnp.broadcast_to(jnp.arange(REQ_DEV, dtype=jnp.int32)[None, :], (N_DP * N_EP, REQ_DEV))
    from_device = from_device.at[device_ids[:, None], send_slot].set(partner)
    from_slot = from_slot.at[device_ids[:, None], send_slot].set(partner_slot)
    return (from_device * REQ_DEV + from_slot).reshape(-1).astype(jnp.int32)


def reference(latent_pool, queries, hidden, lengths, page_table, send_slot, match, routes, route_gain, w_gate, w_up, w_down):
    source = source_rows(send_slot, match)
    page_rows = page_table.reshape(N_DP * N_EP * REQ_DEV, MAXPAGES)
    req_lengths = lengths.reshape(-1)
    key_span = MAXPAGES * PAGE

    def attend(request):
        device = request // REQ_DEV
        pages = page_rows[request] + device * PAGES
        key_cache = latent_pool[pages].reshape(key_span, KV).astype(jnp.float32)
        query_rows = queries[request].reshape(HEADS, KV).astype(jnp.float32)
        scores = jnp.dot(query_rows, key_cache.T, precision=lax.Precision.HIGHEST) * score_scale
        key_valid = jnp.arange(key_span, dtype=jnp.int32) < req_lengths[request]
        scores = jnp.where(key_valid[None, :], scores, -1e30)
        row_max = jnp.max(scores, axis=1, keepdims=True)
        weights = jnp.exp(scores - row_max)
        weights = weights / jnp.sum(weights, axis=1, keepdims=True)
        weights_bf = lax.optimization_barrier(weights.astype(jnp.bfloat16)).astype(jnp.float32)
        context = jnp.dot(weights_bf, key_cache[:, :LATENT], precision=lax.Precision.HIGHEST)
        return context.astype(jnp.bfloat16).reshape(-1)

    attn_context = lax.map(attend, source)
    token_rows = hidden[source]
    gains = route_gain.astype(jnp.float32) * gain_step
    slot_total = N_DP * N_EP * CAP

    def expert_step(total, expert_id):
        named_here = routes == expert_id
        routed_here = jnp.any(named_here, axis=1)
        row_total = jnp.sum(routed_here.astype(jnp.int32))
        chosen = jnp.nonzero(routed_here, size=slot_total, fill_value=0)[0].astype(jnp.int32)
        filled = jnp.arange(slot_total, dtype=jnp.int32) < row_total
        picked = token_rows[chosen]
        gate_proj = jnp.dot(picked, w_gate[expert_id], preferred_element_type=jnp.float32)
        up_proj = jnp.dot(picked, w_up[expert_id], preferred_element_type=jnp.float32)
        activated = (jax.nn.silu(gate_proj) * up_proj).astype(jnp.bfloat16)
        summed = jnp.zeros((slot_total, D), jnp.float32)
        for replica in range(N_DP):
            low = replica * FF_DEV
            partial_out = jnp.dot(activated[:, low:low + FF_DEV], w_down[expert_id, low:low + FF_DEV], preferred_element_type=jnp.float32)
            summed = summed + lax.optimization_barrier(partial_out.astype(jnp.bfloat16)).astype(jnp.float32)
        expert_rows = summed.astype(jnp.bfloat16).astype(jnp.float32)
        weight_now = jnp.sum(jnp.where(named_here, gains, jnp.float32(0.0)), axis=1)[chosen]
        weight_now = jnp.where(filled, weight_now, jnp.float32(0.0))
        return total.at[chosen].add(weight_now[:, None] * expert_rows), None

    total, unused = lax.scan(expert_step, jnp.zeros((N_DP * N_EP * REQ_DEV, D), jnp.float32), jnp.arange(EXPERTS, dtype=jnp.int32))
    return attn_context, total.astype(jnp.bfloat16)
```

```python
import jax
import jax.numpy as jnp
from jax import lax
from jax.sharding import Mesh, PartitionSpec as P

HEADS = 128
ROPE = 64
TOP = 8

score_scale = 192.0 ** (-0.5)
gain_step = 0.0625

ALL = ("yl", "core", "x", "yh", "z")
PEERS = ("yl", "x", "yh", "z")


def flip(value, axes, mask):
    return lax.ppermute(value, axes, [(i, i ^ mask) for i in range(4 if len(axes) == 2 else 2)])


def swapped(rows, flips):
    by_one = flip(rows, ("core",), 1)
    by_two = flip(rows, ("yl",), 1)
    by_three = flip(rows, ("yl", "core"), 3)
    which = flips.reshape((-1,) + (1,) * (rows.ndim - 1))
    return jnp.where(which == 1, by_one, jnp.where(which == 2, by_two, by_three))


def attend(latent_pool, queries, lengths, page_table):
    row_count = queries.shape[0]
    kv_width = queries.shape[1] // HEADS
    latent_width = kv_width - ROPE
    pages = latent_pool.reshape(latent_pool.shape[0], -1, kv_width)
    key_cache = pages[page_table.reshape(-1)].reshape(row_count, -1, kv_width)
    key_span = key_cache.shape[1]
    positions = lax.broadcasted_iota(jnp.int32, (row_count, key_span), 1)
    key_valid = positions < lengths.reshape(row_count, 1)
    query_heads = queries.reshape(row_count, HEADS, kv_width)
    scores = (
        jnp.einsum("rhc,rtc->rht", query_heads, key_cache, preferred_element_type=jnp.float32)
        * score_scale
    )
    scores = jnp.where(key_valid[:, None, :], scores, -1e30)
    row_max = jnp.max(scores, axis=2, keepdims=True)
    weights = jnp.exp(scores - row_max)
    weights = weights / jnp.sum(weights, axis=2, keepdims=True)
    context = jnp.einsum(
        "rht,rtc->rhc",
        weights.astype(jnp.bfloat16),
        key_cache[:, :, :latent_width],
        preferred_element_type=jnp.float32,
    )
    return context.astype(jnp.bfloat16).reshape(row_count, HEADS * latent_width)


def body(
    latent_pool,
    queries,
    hidden,
    lengths,
    page_table,
    send_slot,
    match,
    routes,
    route_gain,
    w_gate,
    w_up,
    w_down,
):
    experts = 32
    row_count = queries.shape[0]
    model_width = hidden.shape[1]
    out_slots = send_slot.reshape(-1)
    flips = match.reshape(-1)

    arriving = swapped(hidden[out_slots], flips)
    slots = jnp.arange(row_count, dtype=jnp.int32)
    leaving = (slots[:, None] == out_slots[None, :]).astype(jnp.float32)
    staying = 1.0 - jnp.sum(leaving, axis=1)

    capacity = min(row_count, max(2, 2 * row_count * TOP // experts))
    expert_ids = jnp.arange(experts, dtype=jnp.int32)
    named = (routes[:, :, None] == expert_ids).astype(jnp.int32)
    chosen = jnp.sum(named, axis=1)
    rank = jnp.cumsum(chosen, axis=0) - chosen
    gain_of = jnp.sum(named * route_gain[:, :, None], axis=1).astype(jnp.float32) * gain_step
    at_slot = (rank[:, :, None] == jnp.arange(capacity, dtype=jnp.int32)) & (chosen[:, :, None] > 0)
    table = at_slot.astype(jnp.float32).reshape(row_count, experts * capacity)
    gain_table = jnp.where(at_slot, gain_of[:, :, None], 0.0).reshape(row_count, experts * capacity)

    picks = jnp.concatenate([table * staying[:, None], jnp.dot(leaving.T, table)], axis=0)
    picks = jnp.concatenate([picks, picks], axis=1).astype(jnp.bfloat16)
    rows = jnp.concatenate([hidden, arriving], axis=0)
    outgoing = lax.dot_general(
        picks, rows, (((0,), (0,)), ((), ())), preferred_element_type=jnp.float32
    )
    outgoing = outgoing.astype(jnp.bfloat16).reshape(2 * experts, capacity, model_width)
    arrived = lax.all_to_all(outgoing, PEERS, split_axis=0, concat_axis=0, tiled=True)
    arrived = arrived.reshape(2 * experts * capacity, model_width)

    gate_other = flip(w_gate[0], ("core",), 1)
    up_other = flip(w_up[0], ("core",), 1)
    down_other = flip(w_down[0], ("core",), 1)

    context = attend(latent_pool, queries, lengths, page_table)

    def units(gate, up):
        gate_proj = jnp.dot(arrived, gate, preferred_element_type=jnp.float32)
        up_proj = jnp.dot(arrived, up, preferred_element_type=jnp.float32)
        return (jax.nn.silu(gate_proj) * up_proj).astype(jnp.bfloat16)

    activated = jnp.concatenate([units(w_gate[0], w_up[0]), units(gate_other, up_other)], axis=1)
    down = jnp.concatenate([w_down[0], down_other], axis=0)
    partial = jnp.dot(activated, down, preferred_element_type=jnp.float32).astype(jnp.bfloat16)
    returned = lax.all_to_all(
        partial.reshape(2 * experts, capacity, model_width),
        PEERS,
        split_axis=0,
        concat_axis=0,
        tiled=True,
    ).reshape(2 * experts * capacity, model_width)
    mix = jnp.concatenate([gain_table, gain_table], axis=1).astype(jnp.bfloat16)
    moe_out = jnp.dot(mix, returned, preferred_element_type=jnp.float32).astype(jnp.bfloat16)

    back = swapped(context[out_slots], flips)
    for k in range(out_slots.shape[0]):
        context = lax.dynamic_update_slice_in_dim(context, back[k : k + 1], out_slots[k], 0)
    return (context, moe_out)


def solution(mesh):
    fine = Mesh(mesh.devices.reshape(2, 2, 4, 2, 4), ALL)
    rows = P(ALL, None)
    column = ("x", "yh", "z")
    replica = ("yl", "core")
    placed = (
        rows,
        rows,
        rows,
        rows,
        rows,
        rows,
        P(column, None),
        rows,
        rows,
        P(column, None, replica),
        P(column, None, replica),
        P(column, replica, None),
    )
    return jax.shard_map(body, mesh=fine, in_specs=placed, out_specs=(rows, rows), check_vma=False)
```

```python
import jax
import jax.numpy as jnp
from jax import lax
from jax.sharding import Mesh, PartitionSpec as P

HEADS = 128
ROPE = 64
TOP = 8

score_scale = 192.0 ** (-0.5)
gain_step = 0.0625

ALL = ("yl", "core", "x", "yh", "z")
PEERS = ("yl", "x", "yh", "z")


def flip(value, axes, mask):
    return lax.ppermute(value, axes, [(i, i ^ mask) for i in range(4 if len(axes) == 2 else 2)])


def swapped(rows, flips):
    by_one = flip(rows, ("core",), 1)
    by_two = flip(rows, ("yl",), 1)
    by_three = flip(rows, ("yl", "core"), 3)
    which = flips.reshape((-1,) + (1,) * (rows.ndim - 1))
    return jnp.where(which == 1, by_one, jnp.where(which == 2, by_two, by_three))


def attend(latent_pool, queries, lengths, page_table):
    row_count = queries.shape[0]
    kv_width = queries.shape[1] // HEADS
    latent_width = kv_width - ROPE
    pages = latent_pool.reshape(latent_pool.shape[0], -1, kv_width)
    key_cache = pages[page_table.reshape(-1)].reshape(row_count, -1, kv_width)
    key_span = key_cache.shape[1]
    positions = lax.broadcasted_iota(jnp.int32, (row_count, key_span), 1)
    key_valid = positions < lengths.reshape(row_count, 1)
    query_heads = queries.reshape(row_count, HEADS, kv_width)
    scores = (
        jnp.einsum("rhc,rtc->rht", query_heads, key_cache, preferred_element_type=jnp.float32)
        * score_scale
    )
    scores = jnp.where(key_valid[:, None, :], scores, -1e30)
    row_max = jnp.max(scores, axis=2, keepdims=True)
    weights = jnp.exp(scores - row_max)
    weights = weights / jnp.sum(weights, axis=2, keepdims=True)
    context = jnp.einsum(
        "rht,rtc->rhc",
        weights.astype(jnp.bfloat16),
        key_cache[:, :, :latent_width],
        preferred_element_type=jnp.float32,
    )
    return context.astype(jnp.bfloat16).reshape(row_count, HEADS * latent_width)


def body(
    latent_pool,
    queries,
    hidden,
    lengths,
    page_table,
    send_slot,
    match,
    routes,
    route_gain,
    w_gate,
    w_up,
    w_down,
):
    experts = 32
    row_count = queries.shape[0]
    model_width = hidden.shape[1]
    out_slots = send_slot.reshape(-1)
    flips = match.reshape(-1)

    arriving = swapped(hidden[out_slots], flips)
    slots = jnp.arange(row_count, dtype=jnp.int32)
    leaving = (slots[:, None] == out_slots[None, :]).astype(jnp.float32)
    staying = 1.0 - jnp.sum(leaving, axis=1)

    capacity = min(row_count, max(2, 2 * row_count * TOP // experts))
    expert_ids = jnp.arange(experts, dtype=jnp.int32)
    named = (routes[:, :, None] == expert_ids).astype(jnp.int32)
    chosen = jnp.sum(named, axis=1)
    rank = jnp.cumsum(chosen, axis=0) - chosen
    gain_of = jnp.sum(named * route_gain[:, :, None], axis=1).astype(jnp.float32) * gain_step
    at_slot = (rank[:, :, None] == jnp.arange(capacity, dtype=jnp.int32)) & (chosen[:, :, None] > 0)
    table = at_slot.astype(jnp.float32).reshape(row_count, experts * capacity)
    gain_table = jnp.where(at_slot, gain_of[:, :, None], 0.0).reshape(row_count, experts * capacity)

    picks = jnp.concatenate([table * staying[:, None], jnp.dot(leaving.T, table)], axis=0)
    picks = jnp.concatenate([picks, picks], axis=1).astype(jnp.bfloat16)
    rows = jnp.concatenate([hidden, arriving], axis=0)
    outgoing = lax.dot_general(
        picks, rows, (((0,), (0,)), ((), ())), preferred_element_type=jnp.float32
    )
    outgoing = outgoing.astype(jnp.bfloat16).reshape(2 * experts, capacity, model_width)
    outgoing, latent_pool, queries = lax.optimization_barrier((outgoing, latent_pool, queries))
    arrived = lax.all_to_all(outgoing, PEERS, split_axis=0, concat_axis=0, tiled=True)
    arrived = arrived.reshape(2 * experts * capacity, model_width)

    gate_other = flip(w_gate[0], ("core",), 1)
    up_other = flip(w_up[0], ("core",), 1)
    down_other = flip(w_down[0], ("core",), 1)

    context = attend(latent_pool, queries, lengths, page_table)
    arrived, context = lax.optimization_barrier((arrived, context))

    def units(gate, up):
        gate_proj = jnp.dot(arrived, gate, preferred_element_type=jnp.float32)
        up_proj = jnp.dot(arrived, up, preferred_element_type=jnp.float32)
        return (jax.nn.silu(gate_proj) * up_proj).astype(jnp.bfloat16)

    activated = jnp.concatenate([units(w_gate[0], w_up[0]), units(gate_other, up_other)], axis=1)
    down = jnp.concatenate([w_down[0], down_other], axis=0)
    partial = jnp.dot(activated, down, preferred_element_type=jnp.float32).astype(jnp.bfloat16)
    returned = lax.all_to_all(
        partial.reshape(2 * experts, capacity, model_width),
        PEERS,
        split_axis=0,
        concat_axis=0,
        tiled=True,
    ).reshape(2 * experts * capacity, model_width)
    mix = jnp.concatenate([gain_table, gain_table], axis=1).astype(jnp.bfloat16)
    moe_out = jnp.dot(mix, returned, preferred_element_type=jnp.float32).astype(jnp.bfloat16)

    back = swapped(context[out_slots], flips)
    for k in range(out_slots.shape[0]):
        context = lax.dynamic_update_slice_in_dim(context, back[k : k + 1], out_slots[k], 0)
    return (context, moe_out)


def solution(mesh):
    fine = Mesh(mesh.devices.reshape(2, 2, 4, 2, 4), ALL)
    rows = P(ALL, None)
    column = ("x", "yh", "z")
    replica = ("yl", "core")
    placed = (
        rows,
        rows,
        rows,
        rows,
        rows,
        rows,
        P(column, None),
        rows,
        rows,
        P(column, None, replica),
        P(column, None, replica),
        P(column, replica, None),
    )
    return jax.shard_map(body, mesh=fine, in_specs=placed, out_specs=(rows, rows), check_vma=False)
```

```python
import jax
import jax.numpy as jnp
from jax import lax
from jax.sharding import Mesh, PartitionSpec as P

HEADS = 128
ROPE = 64
TOP = 8

score_scale = 192.0 ** (-0.5)
gain_step = 0.0625

ALL = ("yl", "core", "x", "yh", "z")
PEERS = ("yl", "x", "yh", "z")


def flip(value, axes, mask):
    return lax.ppermute(value, axes, [(i, i ^ mask) for i in range(4 if len(axes) == 2 else 2)])


def swapped(rows, flips):
    by_one = flip(rows, ("core",), 1)
    by_two = flip(rows, ("yl",), 1)
    by_three = flip(rows, ("yl", "core"), 3)
    which = flips.reshape((-1,) + (1,) * (rows.ndim - 1))
    return jnp.where(which == 1, by_one, jnp.where(which == 2, by_two, by_three))


def attend(latent_pool, queries, lengths, page_table):
    row_count = queries.shape[0]
    kv_width = queries.shape[1] // HEADS
    latent_width = kv_width - ROPE
    pages = latent_pool.reshape(latent_pool.shape[0], -1, kv_width)
    key_cache = pages[page_table.reshape(-1)].reshape(row_count, -1, kv_width)
    key_span = key_cache.shape[1]
    positions = lax.broadcasted_iota(jnp.int32, (row_count, key_span), 1)
    key_valid = positions < lengths.reshape(row_count, 1)
    query_heads = queries.reshape(row_count, HEADS, kv_width)
    scores = (
        jnp.einsum("rhc,rtc->rht", query_heads, key_cache, preferred_element_type=jnp.float32)
        * score_scale
    )
    scores = jnp.where(key_valid[:, None, :], scores, -1e30)
    row_max = jnp.max(scores, axis=2, keepdims=True)
    weights = jnp.exp(scores - row_max)
    weights = weights / jnp.sum(weights, axis=2, keepdims=True)
    context = jnp.einsum(
        "rht,rtc->rhc",
        weights.astype(jnp.bfloat16),
        key_cache[:, :, :latent_width],
        preferred_element_type=jnp.float32,
    )
    return context.astype(jnp.bfloat16).reshape(row_count, HEADS * latent_width)


def body(
    latent_pool,
    queries,
    hidden,
    lengths,
    page_table,
    send_slot,
    match,
    routes,
    route_gain,
    w_gate,
    w_up,
    w_down,
):
    experts = 32
    row_count = queries.shape[0]
    model_width = hidden.shape[1]
    out_slots = send_slot.reshape(-1)
    flips = match.reshape(-1)

    arriving = swapped(hidden[out_slots], flips)
    slots = jnp.arange(row_count, dtype=jnp.int32)
    leaving = (slots[:, None] == out_slots[None, :]).astype(jnp.float32)
    staying = 1.0 - jnp.sum(leaving, axis=1)

    capacity = min(row_count, max(2, 2 * row_count * TOP // experts))
    expert_ids = jnp.arange(experts, dtype=jnp.int32)
    named = (routes[:, :, None] == expert_ids).astype(jnp.int32)
    chosen = jnp.sum(named, axis=1)
    rank = jnp.cumsum(chosen, axis=0) - chosen
    gain_of = jnp.sum(named * route_gain[:, :, None], axis=1).astype(jnp.float32) * gain_step
    at_slot = (rank[:, :, None] == jnp.arange(capacity, dtype=jnp.int32)) & (chosen[:, :, None] > 0)
    table = at_slot.astype(jnp.float32).reshape(row_count, experts * capacity)
    gain_table = jnp.where(at_slot, gain_of[:, :, None], 0.0).reshape(row_count, experts * capacity)

    half = capacity // 2
    places = 2 * experts * half
    rows = jnp.concatenate([hidden, arriving], axis=0)

    def part(of_slots, c):
        cut = of_slots.reshape(row_count, experts, 2, half)[:, :, c]
        cut = cut.reshape(row_count, experts * half)
        return jnp.concatenate([cut, cut], axis=1)

    def leave(c):
        cut = part(table, c)
        picks = jnp.concatenate([cut * staying[:, None], jnp.dot(leaving.T, cut)], axis=0)
        out = lax.dot_general(
            picks.astype(jnp.bfloat16),
            rows,
            (((0,), (0,)), ((), ())),
            preferred_element_type=jnp.float32,
        )
        return out.astype(jnp.bfloat16).reshape(2 * experts, half, model_width)

    def exchange(blocks):
        return lax.all_to_all(blocks, PEERS, split_axis=0, concat_axis=0, tiled=True)

    gate_other = flip(w_gate[0], ("core",), 1)
    up_other = flip(w_up[0], ("core",), 1)
    down = jnp.concatenate([w_down[0], flip(w_down[0], ("core",), 1)], axis=0)

    def expert(blocks):
        block_rows = blocks.reshape(places, model_width)

        def units(gate, up):
            gate_proj = jnp.dot(block_rows, gate, preferred_element_type=jnp.float32)
            up_proj = jnp.dot(block_rows, up, preferred_element_type=jnp.float32)
            return (jax.nn.silu(gate_proj) * up_proj).astype(jnp.bfloat16)

        activated = jnp.concatenate(
            [units(w_gate[0], w_up[0]), units(gate_other, up_other)], axis=1
        )
        partial = jnp.dot(activated, down, preferred_element_type=jnp.float32)
        return partial.astype(jnp.bfloat16).reshape(2 * experts, half, model_width)

    def mixed(blocks, c):
        mix = part(gain_table, c).astype(jnp.bfloat16)
        return jnp.dot(
            mix, blocks.reshape(places, model_width), preferred_element_type=jnp.float32
        )

    leave0 = leave(0)
    leave1 = leave(1)
    leave0, latent_pool, queries = lax.optimization_barrier((leave0, latent_pool, queries))
    come0 = exchange(leave0)
    context = attend(latent_pool, queries, lengths, page_table)
    come0, leave1 = lax.optimization_barrier((come0, leave1))
    come1 = exchange(leave1)
    back0 = expert(come0)
    come1, back0, context = lax.optimization_barrier((come1, back0, context))
    final0 = exchange(back0)
    back1 = expert(come1)
    final0, back1 = lax.optimization_barrier((final0, back1))
    final1 = exchange(back1)
    moe_out = (mixed(final0, 0) + mixed(final1, 1)).astype(jnp.bfloat16)

    back = swapped(context[out_slots], flips)
    for k in range(out_slots.shape[0]):
        context = lax.dynamic_update_slice_in_dim(context, back[k : k + 1], out_slots[k], 0)
    return (context, moe_out)


def solution(mesh):
    fine = Mesh(mesh.devices.reshape(2, 2, 4, 2, 4), ALL)
    rows = P(ALL, None)
    column = ("x", "yh", "z")
    replica = ("yl", "core")
    placed = (
        rows,
        rows,
        rows,
        rows,
        rows,
        rows,
        P(column, None),
        rows,
        rows,
        P(column, None, replica),
        P(column, None, replica),
        P(column, replica, None),
    )
    return jax.shard_map(body, mesh=fine, in_specs=placed, out_specs=(rows, rows), check_vma=False)
```

```python
import jax
import jax.numpy as jnp
from jax import lax
from jax.experimental import pallas as pl
from jax.experimental.pallas import tpu as pltpu
from jax.sharding import Mesh, PartitionSpec as P

HEADS = 128
ROPE = 64
TOP = 8
OUT_A = 3584
BACK_A = 3584
STEP = 896

score_scale = 192.0 ** (-0.5)
gain_step = 0.0625

ALL = ("yl", "core", "x", "yh", "z")
PEERS = ("yl", "x", "yh", "z")


def flip(value, axes, mask):
    return lax.ppermute(value, axes, [(i, i ^ mask) for i in range(4 if len(axes) == 2 else 2)])


def swapped(rows, flips):
    by_one = flip(rows, ("core",), 1)
    by_two = flip(rows, ("yl",), 1)
    by_three = flip(rows, ("yl", "core"), 3)
    which = flips.reshape((-1,) + (1,) * (rows.ndim - 1))
    return jnp.where(which == 1, by_one, jnp.where(which == 2, by_two, by_three))


def pairs_of(latent_pool, page_table, row_count, kv_width):
    pages = latent_pool.reshape(latent_pool.shape[0], -1, 2 * kv_width)
    return pages[page_table.reshape(-1)].reshape(row_count, -1, 2 * kv_width)


def halves(pairs, kv_width):
    wide = -(-kv_width // 128) * 128
    return pairs[:, :, :wide], pairs[:, :, 2 * kv_width - wide :]


def probabilities(pairs, query_heads, lengths):
    row_count, _, kv_width = query_heads.shape
    even, odd = halves(pairs, kv_width)
    extra = ((0, 0), (0, 0), (0, even.shape[2] - kv_width))
    at = 2 * lax.broadcasted_iota(jnp.int32, (1, 1, pairs.shape[1]), 2)
    length = lengths.reshape(row_count, 1, 1)

    def scores_of(keys, padded, at):
        scores = jnp.einsum("rhc,rtc->rht", padded, keys, preferred_element_type=jnp.float32)
        return jnp.where(at < length, scores * score_scale, -1e30)

    scores_even = scores_of(even, jnp.pad(query_heads, extra), at)
    scores_odd = scores_of(odd, jnp.pad(query_heads, [pad[::-1] for pad in extra]), at + 1)
    row_max = jnp.maximum(
        jnp.max(scores_even, axis=2, keepdims=True), jnp.max(scores_odd, axis=2, keepdims=True)
    )
    weights_even, weights_odd = jnp.exp(scores_even - row_max), jnp.exp(scores_odd - row_max)
    total = jnp.sum(weights_even, axis=2, keepdims=True)
    total = total + jnp.sum(weights_odd, axis=2, keepdims=True)
    return (weights_even / total).astype(jnp.bfloat16), (weights_odd / total).astype(jnp.bfloat16)


def contexts(probs, pairs, kv_width):
    row_count = pairs.shape[0]
    latent_width = kv_width - ROPE
    even, odd = halves(pairs, kv_width)
    first = even.shape[2] - kv_width

    def mean(probs, keys):
        return jnp.einsum("rht,rtc->rhc", probs, keys, preferred_element_type=jnp.float32)

    context = mean(probs[0], even[:, :, :latent_width])
    context = context + mean(probs[1], odd)[:, :, first : first + latent_width]
    return context.astype(jnp.bfloat16).reshape(row_count, HEADS * latent_width)


def finish_kernel(steps, x, gates, ups, shares, downs, back, activated, sums):
    at = pl.program_id(0)

    @pl.when(at == 0)
    def _():
        for total, share in zip(sums, shares):
            total[...] = share[...]

    @pl.when(at < steps)
    def _():
        for total, w in zip(sums, gates + ups):
            total[...] += jnp.dot(x[...], w[...], preferred_element_type=jnp.float32)

    @pl.when(at == steps - 1)
    def _():
        width = sums[0].shape[1]
        for core in range(2):
            unit = jax.nn.silu(sums[core][...]) * sums[2 + core][...]
            activated[:, core * width : (core + 1) * width] = unit.astype(jnp.bfloat16)

    @pl.when(at >= steps)
    def _():
        width = sums[0].shape[1]
        back[...] = (
            jnp.dot(activated[:, :width], downs[0][...], preferred_element_type=jnp.float32)
            + jnp.dot(activated[:, width:], downs[1][...], preferred_element_type=jnp.float32)
        ).astype(jnp.bfloat16)


def finish(come, gates, ups, shares, downs, first, columns):
    places, rest = come.shape
    units = gates[0].shape[1]
    steps, tail = rest // STEP, columns // STEP

    def kernel(*refs):
        x, *refs = refs
        finish_kernel(
            steps, x, refs[0:2], refs[2:4], refs[4:8], refs[8:10], refs[10], refs[11], refs[12:]
        )

    weight = pl.BlockSpec(
        (STEP, units), lambda i: (first // STEP + jnp.minimum(i, steps - 1), 0)
    )
    share = pl.BlockSpec((places, units), lambda i: (0, 0))
    down = pl.BlockSpec((units, STEP), lambda i: (0, jnp.maximum(i - steps, 0)))
    work = 2 * places * 2 * units
    return pl.pallas_call(
        kernel,
        grid=(steps + tail,),
        in_specs=[pl.BlockSpec((places, STEP), lambda i: (0, jnp.minimum(i, steps - 1)))]
        + [weight] * 4
        + [share] * 4
        + [down] * 2,
        out_specs=[
            pl.BlockSpec((places, STEP), lambda i: (0, jnp.maximum(i - steps, 0))),
            pl.BlockSpec((places, 2 * units), lambda i: (0, 0)),
        ],
        out_shape=[
            jax.ShapeDtypeStruct((places, columns), jnp.bfloat16),
            jax.ShapeDtypeStruct((places, 2 * units), jnp.bfloat16),
        ],
        scratch_shapes=[pltpu.VMEM((places, units), jnp.float32)] * 4,
        compiler_params=pltpu.CompilerParams(vmem_limit_bytes=58 * 1024 * 1024),
        cost_estimate=pl.CostEstimate(
            flops=work * (2 * rest + columns),
            bytes_accessed=2 * (rest * (places + 4 * units) + columns * (places + 2 * units)),
            transcendentals=2 * places * units,
        ),
    )(come, *gates, *ups, *shares, *downs)


def body(
    latent_pool,
    queries,
    hidden,
    lengths,
    page_table,
    send_slot,
    match,
    routes,
    route_gain,
    w_gate,
    w_up,
    w_down,
):
    experts = 32
    row_count = queries.shape[0]
    model_width = hidden.shape[1]
    out_slots = send_slot.reshape(-1)
    flips = match.reshape(-1)

    arriving = swapped(hidden[out_slots], flips)
    slots = jnp.arange(row_count, dtype=jnp.int32)
    leaving = (slots[:, None] == out_slots[None, :]).astype(jnp.float32)
    staying = 1.0 - jnp.sum(leaving, axis=1)

    capacity = min(row_count, max(2, 2 * row_count * TOP // experts))
    expert_ids = jnp.arange(experts, dtype=jnp.int32)
    named = (routes[:, :, None] == expert_ids).astype(jnp.int32)
    chosen = jnp.sum(named, axis=1)
    rank = jnp.cumsum(chosen, axis=0) - chosen
    gain_of = jnp.sum(named * route_gain[:, :, None], axis=1).astype(jnp.float32) * gain_step
    at_slot = (rank[:, :, None] == jnp.arange(capacity, dtype=jnp.int32)) & (chosen[:, :, None] > 0)
    table = at_slot.astype(jnp.float32).reshape(row_count, experts * capacity)
    gain_table = jnp.where(at_slot, gain_of[:, :, None], 0.0).reshape(row_count, experts * capacity)

    places = 2 * experts * capacity
    picks = jnp.concatenate([table * staying[:, None], jnp.dot(leaving.T, table)], axis=0)
    picks = jnp.concatenate([picks, picks], axis=1).astype(jnp.bfloat16)
    rows = jnp.concatenate([hidden, arriving], axis=0)

    def leave(cut):
        out = lax.dot_general(
            picks, cut, (((0,), (0,)), ((), ())), preferred_element_type=jnp.float32
        )
        return out.astype(jnp.bfloat16)

    def exchange(blocks):
        blocks = blocks.reshape(2 * experts, capacity, -1)
        out = lax.all_to_all(blocks, PEERS, split_axis=0, concat_axis=0, tiled=True)
        return out.reshape(places, -1)

    def product(a, b):
        return jnp.dot(a, b, preferred_element_type=jnp.float32)

    gates = (w_gate[0], flip(w_gate[0], ("core",), 1))
    ups = (w_up[0], flip(w_up[0], ("core",), 1))
    downs = (w_down[0], flip(w_down[0], ("core",), 1))
    mix = jnp.concatenate([gain_table, gain_table], axis=1).astype(jnp.bfloat16)

    kv_width = queries.shape[1] // HEADS
    leave_a = leave(rows[:, :OUT_A])
    leave_a, latent_pool, queries = lax.optimization_barrier((leave_a, latent_pool, queries))
    come_a = exchange(leave_a)
    leave_b = leave(rows[:, OUT_A:])
    pairs = pairs_of(latent_pool, page_table, row_count, kv_width)
    query_heads = queries.reshape(row_count, HEADS, kv_width)
    come_a, leave_b = lax.optimization_barrier((come_a, leave_b))
    come_b = exchange(leave_b)
    shares = [product(come_a, w[:OUT_A]) for w in gates + ups]
    probs = probabilities(pairs, query_heads, lengths)
    context = contexts(probs, pairs, kv_width)
    moving = context[out_slots]
    come_b, shares, context, moving = lax.optimization_barrier((come_b, shares, context, moving))
    back_a, activated = finish(come_b, gates, ups, shares, downs, OUT_A, BACK_A)
    back_a, activated = lax.optimization_barrier((back_a, activated))
    final_a = exchange(back_a)
    joined = jnp.concatenate([w[:, BACK_A:] for w in downs], axis=0)
    back_b = product(activated, joined).astype(jnp.bfloat16)
    back = swapped(moving, flips)
    final_a, back_b, context, back = lax.optimization_barrier((final_a, back_b, context, back))
    final_b = exchange(back_b)
    for k in range(out_slots.shape[0]):
        context = lax.dynamic_update_slice_in_dim(context, back[k : k + 1], out_slots[k], 0)
    moe_a = product(mix, final_a).astype(jnp.bfloat16)
    moe_b = product(mix, final_b).astype(jnp.bfloat16)
    return (context, jnp.concatenate([moe_a, moe_b], axis=1))


def solution(mesh):
    fine = Mesh(mesh.devices.reshape(2, 2, 4, 2, 4), ALL)
    rows = P(ALL, None)
    column = ("x", "yh", "z")
    replica = ("yl", "core")
    placed = (
        rows,
        rows,
        rows,
        rows,
        rows,
        rows,
        P(column, None),
        rows,
        rows,
        P(column, None, replica),
        P(column, None, replica),
        P(column, replica, None),
    )
    return jax.shard_map(body, mesh=fine, in_specs=placed, out_specs=(rows, rows), check_vma=False)
```

```python
import jax
import jax.numpy as jnp
from jax import lax
from jax.experimental import pallas as pl
from jax.experimental.pallas import tpu as pltpu
from jax.sharding import Mesh, PartitionSpec as P

HEADS = 128
ROPE = 64
EXPERTS = 32
CAP = 8
SIDE = 4
PART_A = 3584
LISTS = 128
STEP = 1792
TAIL_STEP = 896

score_scale = 192.0 ** (-0.5)
gain_step = 0.0625

ALL = ("yl", "core", "x", "yh", "z")
Y = ("yl", "yh")
PLANE = ("x", "z")


def flip(value, axes, mask):
    return lax.ppermute(value, axes, [(i, i ^ mask) for i in range(4 if len(axes) == 2 else 2)])


def swapped(rows, flips):
    by_one = flip(rows, ("core",), 1)
    by_two = flip(rows, ("yl",), 1)
    by_three = flip(rows, ("yl", "core"), 3)
    which = flips.reshape((-1,) + (1,) * (rows.ndim - 1))
    return jnp.where(which == 1, by_one, jnp.where(which == 2, by_two, by_three))


def shift(value, axis, by):
    index = (0, 2, 1, 3) if axis == Y else (0, 1, 2, 3)
    return lax.ppermute(value, axis, [(index[i], index[(i + by) % SIDE]) for i in range(SIDE)])


def gather(value, axis):
    return jnp.stack([value] + [shift(value, axis, s) for s in range(1, SIDE)])


def scatter_sum(blocks, axis):
    total = blocks[0].astype(jnp.float32)
    for s in range(1, SIDE):
        total = total + shift(blocks[s], axis, SIDE - s).astype(jnp.float32)
    return total


def product(a, b):
    return jnp.dot(a, b, preferred_element_type=jnp.float32)


def pairs_of(latent_pool, kv_width):
    return latent_pool.reshape(latent_pool.shape[0], -1, 2 * kv_width)


def halves(pairs, kv_width):
    wide = -(-kv_width // 128) * 128
    return pairs[:, :, :wide], pairs[:, :, 2 * kv_width - wide :]


def probabilities(pairs, query_heads, lengths):
    row_count, _, kv_width = query_heads.shape
    even, odd = halves(pairs, kv_width)
    extra = ((0, 0), (0, 0), (0, even.shape[2] - kv_width))
    at = 2 * lax.broadcasted_iota(jnp.int32, (1, 1, pairs.shape[1]), 2)
    length = lengths.reshape(row_count, 1, 1)

    def scores_of(keys, padded, at):
        scores = jnp.einsum("rhc,rtc->rht", padded, keys, preferred_element_type=jnp.float32)
        return jnp.where(at < length, scores * score_scale, -1e30)

    scores_even = scores_of(even, jnp.pad(query_heads, extra), at)
    scores_odd = scores_of(odd, jnp.pad(query_heads, [pad[::-1] for pad in extra]), at + 1)
    row_max = jnp.maximum(
        jnp.max(scores_even, axis=2, keepdims=True), jnp.max(scores_odd, axis=2, keepdims=True)
    )
    weights_even, weights_odd = jnp.exp(scores_even - row_max), jnp.exp(scores_odd - row_max)
    total = jnp.sum(weights_even, axis=2, keepdims=True)
    total = total + jnp.sum(weights_odd, axis=2, keepdims=True)
    return (weights_even / total).astype(jnp.bfloat16), (weights_odd / total).astype(jnp.bfloat16)


def contexts(probs, pairs, kv_width):
    row_count = pairs.shape[0]
    latent_width = kv_width - ROPE
    even, odd = halves(pairs, kv_width)
    first = even.shape[2] - kv_width

    def mean(probs, keys):
        return jnp.einsum("rht,rtc->rhc", probs, keys, preferred_element_type=jnp.float32)

    context = mean(probs[0], even[:, :, :latent_width])
    context = context + mean(probs[1], odd)[:, :, first : first + latent_width]
    return context.astype(jnp.bfloat16).reshape(row_count, HEADS * latent_width)


def finish_kernel(steps, x, gates, ups, shares, downs, back, activated, sums):
    at = pl.program_id(0)

    @pl.when(at == 0)
    def _():
        for total, share in zip(sums, shares):
            total[...] = share[...]

    @pl.when(at < steps)
    def _():
        for total, w in zip(sums, gates + ups):
            total[...] += jnp.dot(x[...], w[...], preferred_element_type=jnp.float32)

    @pl.when(at == steps - 1)
    def _():
        width = sums[0].shape[1]
        for core in range(2):
            unit = jax.nn.silu(sums[core][...]) * sums[2 + core][...]
            activated[:, core * width : (core + 1) * width] = unit.astype(jnp.bfloat16)

    @pl.when(at >= steps)
    def _():
        width = sums[0].shape[1]
        back[...] = (
            jnp.dot(activated[:, :width], downs[0][...], preferred_element_type=jnp.float32)
            + jnp.dot(activated[:, width:], downs[1][...], preferred_element_type=jnp.float32)
        ).astype(jnp.bfloat16)


def finish(come, gates, ups, shares, downs, first, columns):
    places, rest = come.shape
    units = gates[0].shape[1]
    steps, tail = rest // STEP, columns // TAIL_STEP

    def kernel(*refs):
        x, *refs = refs
        finish_kernel(
            steps, x, refs[0:2], refs[2:4], refs[4:8], refs[8:10], refs[10], refs[11], refs[12:]
        )

    weight = pl.BlockSpec(
        (STEP, units), lambda i: (first // STEP + jnp.minimum(i, steps - 1), 0)
    )
    share = pl.BlockSpec((places, units), lambda i: (0, 0))
    down = pl.BlockSpec((units, TAIL_STEP), lambda i: (0, jnp.maximum(i - steps, 0)))
    work = 2 * places * 2 * units
    return pl.pallas_call(
        kernel,
        grid=(steps + tail,),
        in_specs=[pl.BlockSpec((places, STEP), lambda i: (0, jnp.minimum(i, steps - 1)))]
        + [weight] * 4
        + [share] * 4
        + [down] * 2,
        out_specs=[
            pl.BlockSpec((places, TAIL_STEP), lambda i: (0, jnp.maximum(i - steps, 0))),
            pl.BlockSpec((places, 2 * units), lambda i: (0, 0)),
        ],
        out_shape=[
            jax.ShapeDtypeStruct((places, columns), jnp.bfloat16),
            jax.ShapeDtypeStruct((places, 2 * units), jnp.bfloat16),
        ],
        scratch_shapes=[pltpu.VMEM((places, units), jnp.float32)] * 4,
        compiler_params=pltpu.CompilerParams(vmem_limit_bytes=58 * 1024 * 1024),
        cost_estimate=pl.CostEstimate(
            flops=work * (2 * rest + columns),
            bytes_accessed=2 * (rest * (places + 4 * units) + columns * (places + 2 * units)),
            transcendentals=2 * places * units,
        ),
    )(come, *gates, *ups, *shares, *downs)


def exchange(blocks):
    return lax.all_to_all(blocks, PLANE, split_axis=0, concat_axis=0, tiled=True)


def body(
    latent_pool,
    queries,
    hidden,
    lengths,
    page_table,
    send_slot,
    match,
    routes,
    route_gain,
    w_gate,
    w_up,
    w_down,
):
    row_count, model_width = hidden.shape
    part_b = model_width - PART_A
    kv_width = queries.shape[1] // HEADS
    out_slots = send_slot.reshape(-1)
    flips = match.reshape(-1)
    at_y = lax.axis_index("yh") * 2 + lax.axis_index("yl")

    arriving = swapped(hidden[out_slots], flips)
    slots = jnp.arange(row_count, dtype=jnp.int32)
    token_rows = hidden
    for k in range(out_slots.shape[0]):
        token_rows = jnp.where((slots == out_slots[k])[:, None], arriving[k], token_rows)

    named = (routes[:, :, None] == jnp.arange(EXPERTS, dtype=jnp.int32)).astype(jnp.int32)
    chosen = jnp.sum(named, axis=1)
    place = jnp.cumsum(chosen, axis=0) * chosen
    gain = jnp.sum(named * route_gain[:, :, None], axis=1)
    lists = jnp.concatenate(
        [place, gain, jnp.zeros((row_count, LISTS - 2 * EXPERTS), jnp.int32)], axis=1
    ).astype(jnp.bfloat16)

    send_b = jnp.concatenate([token_rows[:, PART_A:], lists], axis=1)
    send_b = jnp.broadcast_to(send_b, (SIDE * SIDE,) + send_b.shape)
    gate_other = flip(w_gate[0], ("core",), 1)
    up_other = flip(w_up[0], ("core",), 1)
    send_b, gate_other, up_other = lax.optimization_barrier((send_b, gate_other, up_other))
    rows_b = exchange(send_b)
    rows_a = gather(jnp.concatenate([token_rows[:, :PART_A], lists], axis=1), Y)
    rows_a = rows_a.reshape(SIDE * row_count, PART_A + LISTS)
    rows_a, latent_pool = lax.optimization_barrier((rows_a, latent_pool))
    pages = pairs_of(latent_pool, kv_width)
    down_other = flip(w_down[0], ("core",), 1)

    def listed(rows, width, yh):
        lists = rows[:, width:].astype(jnp.float32)
        out = []
        for c in range(2):
            cut = lists[:, c * EXPERTS : (c + 1) * EXPERTS].reshape(-1, SIDE, 2, SIDE)
            out.append(jnp.where(yh == 0, cut[:, :, 0], cut[:, :, 1]))
        return out

    numbers = jnp.arange(1, CAP + 1, dtype=jnp.float32)

    place_a, gain_a = listed(rows_a, PART_A, lax.axis_index("yh"))
    source = jnp.arange(SIDE * row_count, dtype=jnp.int32) // row_count
    own = source[:, None] == jnp.arange(SIDE, dtype=jnp.int32)
    hit_a = (place_a[:, :, :, None, None] == numbers) & own[:, None, None, :, None]
    hit_a = hit_a.reshape(SIDE * row_count, -1)
    weight_a = jnp.broadcast_to(
        gain_a[:, :, :, None], (SIDE * row_count, SIDE, SIDE, SIDE * CAP)
    ).reshape(SIDE * row_count, -1)
    mix_a = jnp.where(hit_a, weight_a * gain_step, 0.0).astype(jnp.bfloat16)
    send_a = lax.dot_general(
        hit_a.astype(jnp.bfloat16),
        rows_a[:, :PART_A],
        (((0,), (0,)), ((), ())),
        preferred_element_type=jnp.float32,
    ).astype(jnp.bfloat16)
    send_a = send_a.reshape(SIDE * SIDE, SIDE * CAP, PART_A)
    send_a, rows_b, pages, queries, down_other = lax.optimization_barrier(
        (send_a, rows_b, pages, queries, down_other)
    )
    come_a = exchange(send_a).reshape(-1, PART_A)

    rows_b = rows_b.reshape(-1, part_b + LISTS)
    source = jnp.arange(SIDE * SIDE * row_count, dtype=jnp.int32) // row_count
    here = source[:, None] == jnp.arange(SIDE * SIDE, dtype=jnp.int32)
    sides = jnp.arange(SIDE, dtype=jnp.int32)
    at_column = (sides[:, None] == lax.axis_index("x")) & (sides == lax.axis_index("z"))
    both = []
    for yh in range(2):
        place_b, gain_b = listed(rows_b, part_b, yh)
        place_b = jnp.sum(jnp.where(at_column, place_b, 0.0), axis=(1, 2))
        gain_b = jnp.sum(jnp.where(at_column, gain_b, 0.0), axis=(1, 2))
        hit = here[:, :, None] & (place_b[:, None, None] == numbers)
        hit = hit.reshape(source.shape[0], -1)
        both.append((hit, jnp.where(hit, gain_b[:, None] * gain_step, 0.0)))
    columns_b, mixes_b = [], []
    for k in range(SIDE):
        low = (at_y + k) % SIDE < 2
        columns_b.append(jnp.where(low, both[0][0], both[1][0]).astype(jnp.bfloat16))
        mixes_b.append(jnp.where(low, both[0][1], both[1][1]).astype(jnp.bfloat16))
    come_b = []
    for k in (1, 3, 2, 0):
        block = lax.dot_general(
            columns_b[k],
            rows_b[:, :part_b],
            (((0,), (0,)), ((), ())),
            preferred_element_type=jnp.float32,
        ).astype(jnp.bfloat16)
        come_b.append(block if k == 0 else shift(block, Y, k))
    come_b = [come_b[i] for i in (3, 0, 2, 1)]
    come_b = jnp.stack([block.reshape(SIDE * SIDE, CAP, part_b) for block in come_b], axis=1)
    come_b = come_b.reshape(-1, part_b)

    gates, ups, downs = (w_gate[0], gate_other), (w_up[0], up_other), (w_down[0], down_other)
    joined = jnp.concatenate([w[:, PART_A:] for w in downs], axis=0)
    shares = [product(come_b, w[PART_A:]) for w in gates + ups]

    pairs = pages[page_table.reshape(-1)].reshape(row_count, -1, 2 * kv_width)
    query_heads = queries.reshape(row_count, HEADS, kv_width)
    come_a, shares, joined, pairs, query_heads = lax.optimization_barrier(
        (come_a, shares, joined, pairs, query_heads)
    )
    back_a, activated = finish(come_a, gates, ups, shares, downs, 0, PART_A)
    back_a, activated, pairs, query_heads = lax.optimization_barrier(
        (back_a, activated, pairs, query_heads)
    )

    final_a = exchange(back_a.reshape(SIDE * SIDE, SIDE * CAP, PART_A)).reshape(-1, PART_A)

    by_source = activated.reshape(SIDE * SIDE, SIDE, CAP, -1)
    final_b = []
    for s in (1, 3, 2, 0):
        block = by_source[:, s].reshape(SIDE * SIDE * CAP, -1)
        block = product(block, joined).astype(jnp.bfloat16)
        final_b.append(block if s == 0 else shift(block, Y, SIDE - s))
    final_b = jnp.concatenate([final_b[i] for i in (3, 0, 2, 1)], axis=0)
    mix_b = jnp.concatenate(mixes_b, axis=1)
    moe_b = product(mix_b, final_b).astype(jnp.bfloat16)
    moe_b = moe_b.reshape(SIDE * SIDE, row_count, part_b)
    probs = probabilities(pairs, query_heads, lengths)
    context = contexts(probs, pairs, kv_width)
    final_a, moe_b, context = lax.optimization_barrier((final_a, moe_b, context))
    moe_b = jnp.sum(exchange(moe_b).astype(jnp.float32), axis=0).astype(jnp.bfloat16)
    moe_a = product(mix_a, final_a).astype(jnp.bfloat16)
    moe_a = scatter_sum(moe_a.reshape(SIDE, row_count, PART_A), Y).astype(jnp.bfloat16)
    moe_a, context = lax.optimization_barrier((moe_a, context))
    back = swapped(context[out_slots], flips)
    for k in range(out_slots.shape[0]):
        context = lax.dynamic_update_slice_in_dim(context, back[k : k + 1], out_slots[k], 0)
    return (context, jnp.concatenate([moe_a, moe_b], axis=1))


def solution(mesh):
    fine = Mesh(mesh.devices.reshape(2, 2, 4, 2, 4), ALL)
    rows = P(ALL, None)
    column = ("x", "yh", "z")
    replica = ("yl", "core")
    placed = (
        rows,
        rows,
        rows,
        rows,
        rows,
        rows,
        P(column, None),
        rows,
        rows,
        P(column, None, replica),
        P(column, None, replica),
        P(column, replica, None),
    )
    return jax.shard_map(body, mesh=fine, in_specs=placed, out_specs=(rows, rows), check_vma=False)
```

```python
import jax
import jax.numpy as jnp
from jax import lax
from jax.experimental import pallas as pl
from jax.experimental.pallas import tpu as pltpu
from jax.sharding import Mesh, PartitionSpec as P

HEADS = 128
ROPE = 64
EXPERTS = 32
CAP = 8
SIDE = 4
PART_A = 3584
LISTS = 128
STEP = 1792
TAIL_STEP = 896

score_scale = 192.0 ** (-0.5)
gain_step = 0.0625

ALL = ("yl", "core", "x", "yh", "z")
Y = ("yl", "yh")
PLANE = ("x", "z")


def flip(value, axes, mask):
    return lax.ppermute(value, axes, [(i, i ^ mask) for i in range(4 if len(axes) == 2 else 2)])


def swapped(rows, flips):
    by_one = flip(rows, ("core",), 1)
    by_two = flip(rows, ("yl",), 1)
    by_three = flip(rows, ("yl", "core"), 3)
    which = flips.reshape((-1,) + (1,) * (rows.ndim - 1))
    return jnp.where(which == 1, by_one, jnp.where(which == 2, by_two, by_three))


def shift(value, axis, by):
    index = (0, 2, 1, 3) if axis == Y else (0, 1, 2, 3)
    return lax.ppermute(value, axis, [(index[i], index[(i + by) % SIDE]) for i in range(SIDE)])


def gather(value, axis):
    return jnp.stack([value] + [shift(value, axis, s) for s in range(1, SIDE)])


def scatter_sum(blocks, axis):
    total = blocks[0].astype(jnp.float32)
    for s in range(1, SIDE):
        total = total + shift(blocks[s], axis, SIDE - s).astype(jnp.float32)
    return total


def product(a, b):
    return jnp.dot(a, b, preferred_element_type=jnp.float32)


def pairs_of(latent_pool, kv_width):
    return latent_pool.reshape(latent_pool.shape[0], -1, 2 * kv_width)


def halves(pairs, kv_width):
    wide = -(-kv_width // 128) * 128
    return pairs[:, :, :wide], pairs[:, :, 2 * kv_width - wide :]


def probabilities(pairs, query_heads, lengths):
    row_count, _, kv_width = query_heads.shape
    even, odd = halves(pairs, kv_width)
    extra = ((0, 0), (0, 0), (0, even.shape[2] - kv_width))
    at = 2 * lax.broadcasted_iota(jnp.int32, (1, 1, pairs.shape[1]), 2)
    length = lengths.reshape(row_count, 1, 1)

    def scores_of(keys, padded, at):
        scores = jnp.einsum("rhc,rtc->rht", padded, keys, preferred_element_type=jnp.float32)
        return jnp.where(at < length, scores * score_scale, -1e30)

    scores_even = scores_of(even, jnp.pad(query_heads, extra), at)
    scores_odd = scores_of(odd, jnp.pad(query_heads, [pad[::-1] for pad in extra]), at + 1)
    row_max = jnp.maximum(
        jnp.max(scores_even, axis=2, keepdims=True), jnp.max(scores_odd, axis=2, keepdims=True)
    )
    weights_even, weights_odd = jnp.exp(scores_even - row_max), jnp.exp(scores_odd - row_max)
    total = jnp.sum(weights_even, axis=2, keepdims=True)
    total = total + jnp.sum(weights_odd, axis=2, keepdims=True)
    return (weights_even / total).astype(jnp.bfloat16), (weights_odd / total).astype(jnp.bfloat16)


def contexts(probs, pairs, kv_width):
    row_count = pairs.shape[0]
    latent_width = kv_width - ROPE
    even, odd = halves(pairs, kv_width)
    first = even.shape[2] - kv_width

    def mean(probs, keys):
        return jnp.einsum("rht,rtc->rhc", probs, keys, preferred_element_type=jnp.float32)

    context = mean(probs[0], even[:, :, :latent_width])
    context = context + mean(probs[1], odd)[:, :, first : first + latent_width]
    return context.astype(jnp.bfloat16).reshape(row_count, HEADS * latent_width)


def finish_kernel(steps, x, gates, ups, shares, downs, back, activated, sums):
    at = pl.program_id(0)

    @pl.when(at == 0)
    def _():
        for total, share in zip(sums, shares):
            total[...] = share[...]

    @pl.when(at < steps)
    def _():
        for total, w in zip(sums, gates + ups):
            total[...] += jnp.dot(x[...], w[...], preferred_element_type=jnp.float32)

    @pl.when(at == steps - 1)
    def _():
        width = sums[0].shape[1]
        for core in range(2):
            unit = jax.nn.silu(sums[core][...]) * sums[2 + core][...]
            activated[:, core * width : (core + 1) * width] = unit.astype(jnp.bfloat16)

    @pl.when(at >= steps)
    def _():
        width = sums[0].shape[1]
        back[...] = (
            jnp.dot(activated[:, :width], downs[0][...], preferred_element_type=jnp.float32)
            + jnp.dot(activated[:, width:], downs[1][...], preferred_element_type=jnp.float32)
        ).astype(jnp.bfloat16)


def finish(come, gates, ups, shares, downs, first, columns):
    places, rest = come.shape
    units = gates[0].shape[1]
    steps, tail = rest // STEP, columns // TAIL_STEP

    def kernel(*refs):
        x, *refs = refs
        finish_kernel(
            steps, x, refs[0:2], refs[2:4], refs[4:8], refs[8:10], refs[10], refs[11], refs[12:]
        )

    weight = pl.BlockSpec(
        (STEP, units), lambda i: (first // STEP + jnp.minimum(i, steps - 1), 0)
    )
    share = pl.BlockSpec((places, units), lambda i: (0, 0))
    down = pl.BlockSpec((units, TAIL_STEP), lambda i: (0, jnp.maximum(i - steps, 0)))
    work = 2 * places * 2 * units
    return pl.pallas_call(
        kernel,
        grid=(steps + tail,),
        in_specs=[pl.BlockSpec((places, STEP), lambda i: (0, jnp.minimum(i, steps - 1)))]
        + [weight] * 4
        + [share] * 4
        + [down] * 2,
        out_specs=[
            pl.BlockSpec((places, TAIL_STEP), lambda i: (0, jnp.maximum(i - steps, 0))),
            pl.BlockSpec((places, 2 * units), lambda i: (0, 0)),
        ],
        out_shape=[
            jax.ShapeDtypeStruct((places, columns), jnp.bfloat16),
            jax.ShapeDtypeStruct((places, 2 * units), jnp.bfloat16),
        ],
        scratch_shapes=[pltpu.VMEM((places, units), jnp.float32)] * 4,
        compiler_params=pltpu.CompilerParams(vmem_limit_bytes=58 * 1024 * 1024),
        cost_estimate=pl.CostEstimate(
            flops=work * (2 * rest + columns),
            bytes_accessed=2 * (rest * (places + 4 * units) + columns * (places + 2 * units)),
            transcendentals=2 * places * units,
        ),
    )(come, *gates, *ups, *shares, *downs)


def exchange(blocks):
    return lax.all_to_all(blocks, PLANE, split_axis=0, concat_axis=0, tiled=True)


def body(
    latent_pool,
    queries,
    hidden,
    lengths,
    page_table,
    send_slot,
    match,
    routes,
    route_gain,
    w_gate,
    w_up,
    w_down,
):
    row_count, model_width = hidden.shape
    part_b = model_width - PART_A
    kv_width = queries.shape[1] // HEADS
    out_slots = send_slot.reshape(-1)
    flips = match.reshape(-1)
    at_y = lax.axis_index("yh") * 2 + lax.axis_index("yl")

    arriving = swapped(hidden[out_slots], flips)
    slots = jnp.arange(row_count, dtype=jnp.int32)
    token_rows = hidden
    for k in range(out_slots.shape[0]):
        token_rows = jnp.where((slots == out_slots[k])[:, None], arriving[k], token_rows)

    named = (routes[:, :, None] == jnp.arange(EXPERTS, dtype=jnp.int32)).astype(jnp.int32)
    chosen = jnp.sum(named, axis=1)
    place = jnp.cumsum(chosen, axis=0) * chosen
    gain = jnp.sum(named * route_gain[:, :, None], axis=1)
    lists = jnp.concatenate(
        [place, gain, jnp.zeros((row_count, LISTS - 2 * EXPERTS), jnp.int32)], axis=1
    ).astype(jnp.bfloat16)

    send_b = jnp.concatenate([token_rows[:, PART_A:], lists], axis=1)
    send_b = jnp.broadcast_to(send_b, (SIDE * SIDE,) + send_b.shape)
    gate_other = flip(w_gate[0], ("core",), 1)
    up_other = flip(w_up[0], ("core",), 1)
    send_b, gate_other, up_other = lax.optimization_barrier((send_b, gate_other, up_other))
    rows_b = exchange(send_b)
    rows_a = gather(jnp.concatenate([token_rows[:, :PART_A], lists], axis=1), Y)
    rows_a = rows_a.reshape(SIDE * row_count, PART_A + LISTS)
    rows_a, latent_pool = lax.optimization_barrier((rows_a, latent_pool))
    pages = pairs_of(latent_pool, kv_width)
    down_other = flip(w_down[0], ("core",), 1)

    def listed(rows, width, yh):
        lists = rows[:, width:].astype(jnp.float32)
        out = []
        for c in range(2):
            cut = lists[:, c * EXPERTS : (c + 1) * EXPERTS].reshape(-1, SIDE, 2, SIDE)
            out.append(jnp.where(yh == 0, cut[:, :, 0], cut[:, :, 1]))
        return out

    numbers = jnp.arange(1, CAP + 1, dtype=jnp.float32)

    place_a, gain_a = listed(rows_a, PART_A, lax.axis_index("yh"))
    source = jnp.arange(SIDE * row_count, dtype=jnp.int32) // row_count
    own = source[:, None] == jnp.arange(SIDE, dtype=jnp.int32)
    hit_a = (place_a[:, :, :, None, None] == numbers) & own[:, None, None, :, None]
    hit_a = hit_a.reshape(SIDE * row_count, -1)
    weight_a = jnp.broadcast_to(
        gain_a[:, :, :, None], (SIDE * row_count, SIDE, SIDE, SIDE * CAP)
    ).reshape(SIDE * row_count, -1)
    mix_a = jnp.where(hit_a, weight_a * gain_step, 0.0).astype(jnp.bfloat16)
    send_a = lax.dot_general(
        hit_a.astype(jnp.bfloat16),
        rows_a[:, :PART_A],
        (((0,), (0,)), ((), ())),
        preferred_element_type=jnp.float32,
    ).astype(jnp.bfloat16)
    send_a = send_a.reshape(SIDE * SIDE, SIDE * CAP, PART_A)
    send_a, rows_b, pages, queries, down_other = lax.optimization_barrier(
        (send_a, rows_b, pages, queries, down_other)
    )
    come_a = exchange(send_a).reshape(-1, PART_A)

    rows_b = rows_b.reshape(-1, part_b + LISTS)
    source = jnp.arange(SIDE * SIDE * row_count, dtype=jnp.int32) // row_count
    here = source[:, None] == jnp.arange(SIDE * SIDE, dtype=jnp.int32)
    sides = jnp.arange(SIDE, dtype=jnp.int32)
    at_column = (sides[:, None] == lax.axis_index("x")) & (sides == lax.axis_index("z"))
    both = []
    for yh in range(2):
        place_b, gain_b = listed(rows_b, part_b, yh)
        place_b = jnp.sum(jnp.where(at_column, place_b, 0.0), axis=(1, 2))
        gain_b = jnp.sum(jnp.where(at_column, gain_b, 0.0), axis=(1, 2))
        hit = here[:, :, None] & (place_b[:, None, None] == numbers)
        hit = hit.reshape(source.shape[0], -1)
        both.append((hit, jnp.where(hit, gain_b[:, None] * gain_step, 0.0)))
    columns_b, mixes_b = [], []
    for k in range(SIDE):
        low = (at_y + k) % SIDE < 2
        columns_b.append(jnp.where(low, both[0][0], both[1][0]).astype(jnp.bfloat16))
        mixes_b.append(jnp.where(low, both[0][1], both[1][1]).astype(jnp.bfloat16))
    come_b = []
    for k in (1, 3, 2, 0):
        block = lax.dot_general(
            columns_b[k],
            rows_b[:, :part_b],
            (((0,), (0,)), ((), ())),
            preferred_element_type=jnp.float32,
        ).astype(jnp.bfloat16)
        come_b.append(block if k == 0 else shift(block, Y, k))
    come_b = [come_b[i] for i in (3, 0, 2, 1)]
    come_b = jnp.stack([block.reshape(SIDE * SIDE, CAP, part_b) for block in come_b], axis=1)
    come_b = come_b.reshape(-1, part_b)

    gates, ups, downs = (w_gate[0], gate_other), (w_up[0], up_other), (w_down[0], down_other)
    joined = jnp.concatenate([w[:, PART_A:] for w in downs], axis=0)
    shares = [product(come_b, w[PART_A:]) for w in gates + ups]

    pairs = pages[page_table.reshape(-1)].reshape(row_count, -1, 2 * kv_width)
    query_heads = queries.reshape(row_count, HEADS, kv_width)
    come_a, shares, joined, pairs, query_heads = lax.optimization_barrier(
        (come_a, shares, joined, pairs, query_heads)
    )
    back_a, activated = finish(come_a, gates, ups, shares, downs, 0, PART_A)
    back_a, activated, pairs, query_heads = lax.optimization_barrier(
        (back_a, activated, pairs, query_heads)
    )

    final_a = exchange(back_a.reshape(SIDE * SIDE, SIDE * CAP, PART_A)).reshape(-1, PART_A)

    by_source = activated.reshape(SIDE * SIDE, SIDE, CAP, -1)
    final_b = []
    for s in (1, 3, 2, 0):
        block = by_source[:, s].reshape(SIDE * SIDE * CAP, -1)
        block = product(block, joined).astype(jnp.bfloat16)
        final_b.append(block if s == 0 else shift(block, Y, SIDE - s))
    final_b = jnp.concatenate([final_b[i] for i in (3, 0, 2, 1)], axis=0)
    mix_b = jnp.concatenate(mixes_b, axis=1)
    moe_b = product(mix_b, final_b).astype(jnp.bfloat16)
    moe_b = moe_b.reshape(SIDE * SIDE, row_count, part_b)
    probs = probabilities(pairs, query_heads, lengths)
    context = contexts(probs, pairs, kv_width)
    final_a, moe_b, context = lax.optimization_barrier((final_a, moe_b, context))
    moe_b = jnp.sum(exchange(moe_b).astype(jnp.float32), axis=0).astype(jnp.bfloat16)
    moe_a = product(mix_a, final_a).astype(jnp.bfloat16)
    moe_a = scatter_sum(moe_a.reshape(SIDE, row_count, PART_A), Y).astype(jnp.bfloat16)
    back = swapped(context[out_slots], flips)
    for k in range(out_slots.shape[0]):
        context = lax.dynamic_update_slice_in_dim(context, back[k : k + 1], out_slots[k], 0)
    return (context, jnp.concatenate([moe_a, moe_b], axis=1))


def solution(mesh):
    fine = Mesh(mesh.devices.reshape(2, 2, 4, 2, 4), ALL)
    rows = P(ALL, None)
    column = ("x", "yh", "z")
    replica = ("yl", "core")
    placed = (
        rows,
        rows,
        rows,
        rows,
        rows,
        rows,
        P(column, None),
        rows,
        rows,
        P(column, None, replica),
        P(column, None, replica),
        P(column, replica, None),
    )
    return jax.shard_map(body, mesh=fine, in_specs=placed, out_specs=(rows, rows), check_vma=False)
```
